128 devices in a mesh: ctx: 16 (over x_hi, y, core), tp: 8 (over z, x_lo).
Axes of the slice: x: 4 (x_hi: 2, x_lo: 2; x = x_hi * 2 + x_lo), y: 4, z: 4, core: 2. Of those that a mesh axis runs over, the one named last changes fastest.
Arguments:
- activations: bfloat16 [1536, 8, 4096], P('ctx'), may hold values from -100 to 100
- w_query: bfloat16 [4096, 4096], P(None, 'tp'), may hold values from -0.09375 to 0.09375
- w_key: bfloat16 [4096, 4096], P(None, 'tp'), may hold values from -0.09375 to 0.09375
- w_value: bfloat16 [4096, 4096], P(None, 'tp'), may hold values from -0.09375 to 0.09375
- pre_mix: float32 [32, 32], replicated, may hold values from -1 to 1
- post_mix: float32 [32, 32], replicated, may hold values from -1 to 1
- span_place: int32 [32], replicated, may hold values from 0 to 31, each once
Outputs:
- attended: bfloat16 [1536, 8, 4096], P('ctx', 'tp')
The draws below stay inside these ranges and needn't reach their ends.
Inputs may be any that keep to these rules, and one draw needn't show every extreme that they name: `span_place`: every stored span slot holds a different span of the sequence.
All inputs are finite; a program needn't handle non-finite values.
Results may differ from the reference program's by a relative error of at most 0.012.
The reference program's roundings to bfloat16 on the way (of `mixed`) count: a program that leaves them out, or rounds other values in their place, can miss the bound.
Values may be sent and summed in bfloat16 or wider, within the bound.
A program may use at most 192 MiB of HBM per device.

```python
import jax
import jax.numpy as jnp
from jax import lax

D = 4096
HEADS = 32
HD = 128
SPAN = 48
TOKENS = 1536
SEQS = 8
N_CTX = 16


def draw_activations(key, part):
    key = jax.random.fold_in(key, 11)
    return jnp.clip(jax.random.normal(key, (TOKENS, SEQS, D), jnp.float32), -6.0, 6.0).astype(jnp.bfloat16)


def steps_of(stream_key, dims, cuts, smallest, high):
    def one(dim, blocks):
        steps = jax.random.uniform(jax.random.fold_in(jax.random.fold_in(stream_key, 6), dim), (blocks,), jnp.float32, smallest / len(cuts), high / len(cuts))
        return jnp.repeat(jnp.exp(steps), dims[dim] // blocks).reshape((-1,) + (1,) * (len(dims) - dim - 1))

    gain = one(*cuts[0])
    for cut in cuts[1:]:
        gain = gain * one(*cut)
    return gain


def bell_draw(stream_key, shape, spread, most, cuts=(), kind=jnp.bfloat16):
    drawn = jax.random.normal(stream_key, shape, jnp.float32) * spread
    if len(cuts) > 0:
        drawn = steps_of(stream_key, shape, cuts, -0.22, 0.18) * drawn
    return jnp.clip(drawn, min=-most, max=most).astype(kind)


def setup_inputs(seed: int = 0) -> dict:
    seeds = jax.random.split(jax.random.key(seed), 8)
    return {
        "activations": draw_activations(jax.random.fold_in(seeds[7], 71), 0),
        "w_query": bell_draw(seeds[1], (D, HEADS * HD), D ** -0.5, 0.09375, ((1, 8),)),
        "w_key": bell_draw(seeds[2], (D, HEADS * HD), D ** -0.5, 0.09375, ((1, 8),)),
        "w_value": bell_draw(seeds[3], (D, HEADS * HD), D ** -0.5, 0.09375, ((1, 8),)),
        "pre_mix": bell_draw(seeds[4], (HEADS, HEADS), HEADS ** -0.5, 1.0, (), jnp.float32),
        "post_mix": bell_draw(seeds[5], (HEADS, HEADS), HEADS ** -0.5, 1.0, (), jnp.float32),
        "span_place": jax.random.permutation(seeds[6], 2 * N_CTX).astype(jnp.int32),
    }


def stored_positions(row_ids, span_place):
    return span_place[row_ids // SPAN] * SPAN + row_ids % SPAN


def one_sequence(rows, w_query, w_key, w_value, pre_mix, post_mix, positions):
    query = jnp.dot(rows, w_query, preferred_element_type=jnp.float32).astype(jnp.bfloat16)
    key_all = jnp.dot(rows, w_key, preferred_element_type=jnp.float32).astype(jnp.bfloat16)
    value_all = jnp.dot(rows, w_value, preferred_element_type=jnp.float32).astype(jnp.bfloat16)
    key_heads = key_all.reshape(TOKENS, HEADS, HD).astype(jnp.float32)
    value_heads = value_all.reshape(TOKENS, HEADS, HD).astype(jnp.float32)
    score_scale = HD ** -0.5
    highest = lax.Precision.HIGHEST

    def one_block(operands):
        query_block, query_pos = operands
        raw_scores = jnp.einsum("qhd,khd->hqk", query_block.astype(jnp.float32), key_heads, precision=highest) * score_scale
        logits = jnp.einsum("gh,hqk->gqk", pre_mix, raw_scores, precision=highest)
        visible = positions[None, :] <= query_pos[:, None]
        masked = jnp.where(visible[None], logits, -jnp.inf)
        row_max = jnp.max(masked, axis=2, keepdims=True)
        exp_terms = jnp.where(visible[None], jnp.exp(logits - row_max), 0.0)
        row_total = jnp.sum(exp_terms, axis=2, keepdims=True)
        probs = exp_terms / row_total
        mixed = jnp.einsum("fg,gqk->fqk", post_mix, probs, precision=highest).astype(jnp.bfloat16)
        result = jnp.einsum("fqk,kfd->qfd", mixed.astype(jnp.float32), value_heads, precision=highest)
        return result.reshape(SPAN, HEADS * HD).astype(jnp.bfloat16)

    blocks = query.reshape(TOKENS // SPAN, SPAN, HEADS, HD)
    block_pos = positions.reshape(TOKENS // SPAN, SPAN)
    return lax.map(one_block, (blocks, block_pos)).reshape(TOKENS, HEADS * HD)


def reference(activations, w_query, w_key, w_value, pre_mix, post_mix, span_place):
    positions = stored_positions(jnp.arange(TOKENS, dtype=jnp.int32), span_place)
    per_seq = jnp.transpose(activations, (1, 0, 2))

    def run_one(rows):
        return one_sequence(rows, w_query, w_key, w_value, pre_mix, post_mix, positions)

    results = lax.map(run_one, per_seq)
    return jnp.transpose(results, (1, 0, 2))
```

```python
import functools

import jax
import jax.numpy as jnp
from jax import lax
from jax.experimental import pallas as pl
from jax.experimental.pallas import tpu as pltpu
from jax.sharding import PartitionSpec as P

HEADS = 32
HD = 128
SPAN = 48
MODEL = 4096
SEQS = 8
ROWS = 96
TILE = 384
SLAB = 8
SLABS = TILE // SLAB
MIX = HEADS * SLAB
WIDE = 256
HALF = 2048
FLOOR = -1e30
MESH = pl.DeviceIdType.MESH
F32 = jnp.float32
BF16 = jnp.bfloat16

CHUNKS = ((1, 0), (0, 0), (1, 1), (0, 1), (2, 0), (2, 1))


def dot(a, b):
    return jnp.dot(a, b, preferred_element_type=F32)


def split(x):
    high = x.astype(BF16)
    return high, (x - high.astype(F32)).astype(BF16)


def spread_mix(mix, high_ref, low_ref):
    row = lax.broadcasted_iota(jnp.int32, (MIX, HEADS), 0) // SLAB
    col = lax.broadcasted_iota(jnp.int32, (MIX, HEADS), 1)
    pick = jnp.where(row == col, 1.0, 0.0).astype(BF16)
    same = (lax.broadcasted_iota(jnp.int32, (MIX, MIX), 0) % SLAB) == (
        lax.broadcasted_iota(jnp.int32, (MIX, MIX), 1) % SLAB
    )
    for part, ref in zip(split(mix), (high_ref, low_ref)):
        tall = dot(pick, part).astype(BF16)
        full = lax.dot_general(tall, pick, (((1,), (1,)), ((), ())), preferred_element_type=F32)
        ref[...] = jnp.where(same, full, 0.0).astype(BF16)


def kernel(
    act, w_query, w_key, w_value, pre_mix, post_mix, query_pos, key_pos, out,
    act_v, w_v, res, stage, q_buf, k_buf, v_buf, scores, stat, stat_in,
    part, part_in, pre_high, pre_low, post_high, post_low,
    act_sem, w_sem, own_sem, a2a_send, a2a_recv, y_send, y_recv, q_send, q_recv,
    stat_send, stat_recv, p_send, p_recv,
):
    ctx, tp = lax.axis_index("ctx"), lax.axis_index("tp")
    xh, y, core = ctx // 8, (ctx // 2) % 4, ctx % 2
    up = (xh * 8 + ((y + 1) % 4) * 2 + core, tp)
    down = (xh * 8 + ((y + 3) % 4) * 2 + core, tp)
    y_up, y_down = (y + 1) % 4, (y + 3) % 4
    sibling = (ctx + 1 - 2 * core, tp)
    partner = ((1 - xh) * 8 + y * 2 + core, tp)
    diagonal = ((1 - xh) * 8 + y * 2 + 1 - core, tp)
    mine = xh * 2 + core
    sibling_slot = xh * 2 + 1 - core
    partner_slot = (1 - xh) * 2 + core
    diagonal_slot = (1 - xh) * 2 + 1 - core
    peers = [(ctx, (tp + o) % SEQS) for o in range(1, SEQS)]

    weights = (w_query, w_key, w_value)
    buffers = (q_buf, k_buf, v_buf)

    act_copies = []
    for b in range(3):
        rows = pl.ds(b * 32, 32)
        act_copies.append(pltpu.make_async_copy(act.at[rows], act_v.at[rows], act_sem.at[b]))
    w_copies = []
    for n, (kind, j) in enumerate(CHUNKS):
        w_copies.append(
            pltpu.make_async_copy(weights[kind].at[:, pl.ds(j * WIDE, WIDE)], w_v.at[n], w_sem.at[n])
        )
    w_copies[0].start()
    for c in act_copies:
        c.start()
    for c in w_copies[1:]:
        c.start()

    barrier = pltpu.get_barrier_semaphore()
    friends = peers + [up, down, sibling, partner, diagonal]
    for friend in friends:
        pl.semaphore_signal(barrier, inc=1, device_id=friend, device_id_type=MESH)
    pl.semaphore_wait(barrier, len(friends))

    sends = []

    def remote(src, dst, send, recv, to):
        copy = pltpu.make_async_remote_copy(
            src_ref=src, dst_ref=dst, send_sem=send, recv_sem=recv, device_id=to, device_id_type=MESH
        )
        sends.append(copy)
        return copy

    def slot_of(kind):
        return mine if kind == 0 else y

    exchange = {}

    def project(n):
        kind, j = CHUNKS[n]
        w_copies[n].wait()
        for b in range(3):
            if n == 0:
                act_copies[b].wait()
            rows = act_v[b * 32:(b + 1) * 32].reshape(32 * SEQS, MODEL)
            both = dot(rows, w_v[n])
            for i in range(2):
                res[i] = both[:, i * HD:(i + 1) * HD]
            for s in range(SEQS):
                for i in range(2):
                    stage[n, s, b * 32:(b + 1) * 32, i * HD:(i + 1) * HD] = res[
                        i, pl.ds(s, 32, stride=SEQS), :
                    ].astype(BF16)
        here = buffers[kind].at[j, slot_of(kind), :, pl.ds(pl.multiple_of(tp * WIDE, WIDE), WIDE)]
        copies = []
        for o, peer in enumerate(peers):
            copies.append(
                remote(stage.at[n, peer[1]], here, a2a_send.at[n, o], a2a_recv.at[n, o], peer)
            )
            copies[-1].start()
        own = pltpu.make_async_copy(stage.at[n, tp], here, own_sem.at[n])
        own.start()
        exchange[n] = (copies, own)

    def arrived(n):
        copies, own = exchange[n]
        own.wait()
        for c in copies:
            c.wait_recv()

    ring = {}

    def ring_start(n, r):
        kind, j = CHUNKS[n]
        buf = buffers[kind]
        arrived(n)
        a = remote(buf.at[j, y], buf.at[j, y], y_send.at[r, 0], y_recv.at[r, 0], up)
        b = remote(buf.at[j, y], buf.at[j, y], y_send.at[r, 1], y_recv.at[r, 1], down)
        a.start()
        b.start()
        ring[r] = [a, b]

    def ring_forward(n, r):
        kind, j = CHUNKS[n]
        buf = buffers[kind]
        a, b = ring[r]
        a.wait_recv()
        first = buf.at[j, y_down, pl.ds(0, 48)]
        c = remote(first, first, y_send.at[r, 2], y_recv.at[r, 2], up)
        c.start()
        b.wait_recv()
        second = buf.at[j, y_up, pl.ds(48, 48)]
        d = remote(second, second, y_send.at[r, 3], y_recv.at[r, 3], down)
        d.start()
        ring[r] = [c, d]

    def ring_finish(r):
        for c in ring[r]:
            c.wait_recv()

    queries = {}

    def query_start(n):
        _, j = CHUNKS[n]
        arrived(n)
        a = remote(q_buf.at[j, mine], q_buf.at[j, mine], q_send.at[j, 1], q_recv.at[j, 1], partner)
        b = remote(q_buf.at[j, mine], q_buf.at[j, mine], q_send.at[j, 0], q_recv.at[j, 0], sibling)
        a.start()
        b.start()
        queries[j] = [a, b]

    def query_forward(j):
        a, b = queries[j]
        a.wait_recv()
        there = q_buf.at[j, partner_slot]
        c = remote(there, there, q_send.at[j, 2], q_recv.at[j, 2], sibling)
        c.start()
        queries[j] = [b, c]

    def query_finish(j):
        for c in queries[j]:
            c.wait_recv()

    def score(j):
        def one(hh, carry):
            lanes = pl.ds(pl.multiple_of(hh * HD, HD), HD)
            q = q_buf[j, :, :, lanes].reshape(TILE, HD)
            k = k_buf[j, :, :, lanes].reshape(TILE, HD)
            scores[(hh // 2) * 4 + 2 * j + hh % 2] = lax.dot_general(
                q, k, (((1,), (1,)), ((), ())), preferred_element_type=F32
            )
            return carry

        lax.fori_loop(0, HEADS // 2, one, 0)

    lane = lax.broadcasted_iota(jnp.int32, (MIX, 128), 1)

    def softmax(first, last):
        def one(i, carry):
            rows = pl.ds(pl.multiple_of(i * SLAB, SLAB), SLAB)
            x = scores[:, rows, :].reshape(MIX, TILE)
            high, low = split(x)
            logits = dot(pre_high[...], high) + dot(pre_low[...], high) + dot(pre_high[...], low)
            seen = key_pos[...] <= query_pos[rows, :]
            masked = jnp.where(seen[None], logits.reshape(HEADS, SLAB, TILE), FLOOR).reshape(MIX, TILE)
            top = jnp.max(masked, axis=1, keepdims=True)
            e = jnp.exp(masked - top)
            total = jnp.sum(e, axis=1, keepdims=True)
            scores[:, rows, :] = e.reshape(HEADS, SLAB, TILE)
            stat[...] = jnp.where(lane == i, top, jnp.where(lane == i + 64, total, stat[...]))
            return carry

        lax.fori_loop(first, last, one, 0)

    def post(first, last):
        def one(i, carry):
            rows = pl.ds(pl.multiple_of(i * SLAB, SLAB), SLAB)
            weight = jnp.sum(jnp.where(lane == i, stat[...], 0.0), axis=1, keepdims=True)
            probs = (scores[:, rows, :].reshape(MIX, TILE) * weight).astype(BF16)
            mixed = dot(post_high[...], probs) + dot(post_low[...], probs)
            scores[:, rows, :] = mixed.reshape(HEADS, SLAB, TILE)
            return carry

        lax.fori_loop(first, last, one, 0)

    def attend(j):
        def one(hh, carry):
            lanes = pl.ds(pl.multiple_of(hh * HD, HD), HD)
            v = v_buf[j, :, :, lanes].reshape(TILE, HD)
            m = scores[(hh // 2) * 4 + 2 * j + hh % 2].astype(BF16)
            part[j, :, :, lanes] = dot(m, v).reshape(4, ROWS, HD).astype(BF16)
            return carry

        lax.fori_loop(0, HEADS // 2, one, 0)

    partial = {}

    def partial_start(j):
        a = remote(part.at[j, diagonal_slot], part_in.at[j, 0], p_send.at[j, 0], p_recv.at[j, 0], sibling)
        b = remote(part.at[j, sibling_slot], part_in.at[j, 1], p_send.at[j, 1], p_recv.at[j, 1], sibling)
        a.start()
        b.start()
        partial[j] = [a, b]

    def partial_cross(j):
        a, b = partial[j]
        a.wait_recv()
        part[j, partner_slot] = (
            part[j, partner_slot].astype(F32) + part_in[j, 0].astype(F32)
        ).astype(BF16)
        c = remote(part.at[j, partner_slot], part_in.at[j, 2], p_send.at[j, 2], p_recv.at[j, 2], partner)
        c.start()
        partial[j] = [b, c]

    def partial_finish(j):
        for c in partial[j]:
            c.wait_recv()
        done = (
            part[j, mine].astype(F32) + part_in[j, 1].astype(F32) + part_in[j, 2].astype(F32)
        ).astype(BF16)
        for t in range(SEQS):
            out[:, t * 2 * WIDE + j * WIDE:t * 2 * WIDE + (j + 1) * WIDE] = done[:, t * WIDE:(t + 1) * WIDE]

    project(0)
    project(1)
    project(2)
    ring_start(0, 0)
    project(3)
    project(4)
    query_start(1)
    project(5)
    spread_mix(pre_mix[...] * (HD ** -0.5), pre_high, pre_low)
    spread_mix(post_mix[...], post_high, post_low)
    stat[...] = jnp.zeros_like(stat)
    ring_start(2, 1)
    ring_forward(0, 0)
    query_start(3)
    query_forward(0)
    ring_start(4, 2)
    ring_finish(0)
    query_finish(0)
    score(0)
    ring_forward(2, 1)
    query_forward(1)
    ring_start(5, 3)
    ring_finish(1)
    query_finish(1)
    score(1)
    softmax(0, 24)
    ring_forward(4, 2)
    softmax(24, 48)
    ring_forward(5, 3)
    stat_copies = []
    for n, to in enumerate((sibling, partner, diagonal)):
        stat_copies.append(remote(stat, stat_in.at[n], stat_send.at[n], stat_recv.at[n], to))
        stat_copies[-1].start()
    for c in stat_copies:
        c.wait_recv()
    for c in stat_copies:
        c.wait_send()
    del sends[-3:]
    own = stat[...]
    others = [stat_in[n] for n in range(3)]
    top = functools.reduce(jnp.maximum, others, own)
    total = sum(jnp.exp(s - top) * pltpu.roll(s, 64, 1) for s in [own] + others)
    stat[...] = jnp.exp(own - top) / total
    post(0, 48)
    ring_finish(2)
    attend(0)
    partial_start(0)
    ring_finish(3)
    partial_cross(0)
    attend(1)
    partial_start(1)
    partial_cross(1)
    partial_finish(0)
    partial_finish(1)
    for c in sends:
        c.wait_send()


def local(activations, w_query, w_key, w_value, pre_mix, post_mix, span_place):
    ctx = lax.axis_index("ctx")
    xh, y, core = ctx // 8, (ctx // 2) % 4, ctx % 2
    positions = (span_place[:, None] * SPAN + jnp.arange(SPAN, dtype=jnp.int32)[None, :]).reshape(2, 4, 2, ROWS)
    query_pos = lax.dynamic_index_in_dim(positions, y, 1, keepdims=False).reshape(TILE, 1)
    key_pos = lax.dynamic_index_in_dim(positions, xh, 0, keepdims=False)
    key_pos = lax.dynamic_index_in_dim(key_pos, core, 1, keepdims=False).reshape(1, TILE)
    any_spec = pl.BlockSpec(memory_space=pl.ANY)
    vmem = pl.BlockSpec(memory_space=pltpu.VMEM)
    dma = pltpu.SemaphoreType.DMA
    out = pl.pallas_call(
        kernel,
        name="heads",
        out_shape=jax.ShapeDtypeStruct((ROWS, MODEL), BF16),
        in_specs=[any_spec] * 4 + [vmem] * 4,
        out_specs=vmem,
        scratch_shapes=[
            pltpu.VMEM((ROWS, SEQS, MODEL), BF16),
            pltpu.VMEM((6, MODEL, WIDE), BF16),
            pltpu.VMEM((2, 256, HD), F32),
            pltpu.VMEM((6, SEQS, ROWS, WIDE), BF16),
            pltpu.VMEM((2, 4, ROWS, HALF), BF16),
            pltpu.VMEM((2, 4, ROWS, HALF), BF16),
            pltpu.VMEM((2, 4, ROWS, HALF), BF16),
            pltpu.VMEM((HEADS, TILE, TILE), F32),
            pltpu.VMEM((MIX, 128), F32),
            pltpu.VMEM((3, MIX, 128), F32),
            pltpu.VMEM((2, 4, ROWS, HALF), BF16),
            pltpu.VMEM((2, 3, ROWS, HALF), BF16),
            pltpu.VMEM((MIX, MIX), BF16),
            pltpu.VMEM((MIX, MIX), BF16),
            pltpu.VMEM((MIX, MIX), BF16),
            pltpu.VMEM((MIX, MIX), BF16),
            dma((3,)), dma((6,)), dma((6,)),
            dma((6, 7)), dma((6, 7)),
            dma((4, 4)), dma((4, 4)),
            dma((2, 3)), dma((2, 3)),
            dma((3,)), dma((3,)),
            dma((2, 3)), dma((2, 3)),
        ],
        compiler_params=pltpu.CompilerParams(
            collective_id=0, has_side_effects=True, vmem_limit_bytes=60 * 2**20
        ),
        cost_estimate=pl.CostEstimate(flops=30 * 10**9, bytes_accessed=30 * 10**6, transcendentals=5 * 10**6),
    )(activations, w_query, w_key, w_value, pre_mix, post_mix, query_pos, key_pos)
    return out.reshape(ROWS, 1, MODEL)


def solution(mesh):
    placed = (P("ctx", None, None), P(None, "tp"), P(None, "tp"), P(None, "tp"), P(), P(), P())
    return jax.shard_map(
        local, mesh=mesh, in_specs=placed, out_specs=P("ctx", "tp", None), check_vma=False
    )
```

```python
import functools

import jax
import jax.numpy as jnp
from jax import lax
from jax.experimental import pallas as pl
from jax.experimental.pallas import tpu as pltpu
from jax.sharding import PartitionSpec as P

HEADS = 32
HD = 128
SPAN = 48
MODEL = 4096
SEQS = 8
ROWS = 96
TILE = 384
SLAB = 8
SLABS = TILE // SLAB
MIX = HEADS * SLAB
WIDE = 256
HALF = 2048
FLOOR = -1e30
MESH = pl.DeviceIdType.MESH
F32 = jnp.float32
BF16 = jnp.bfloat16

CHUNKS = ((1, 0), (0, 0), (1, 1), (0, 1), (2, 0), (2, 1))


def dot(a, b):
    return jnp.dot(a, b, preferred_element_type=F32)


def split(x):
    high = x.astype(BF16)
    return high, (x - high.astype(F32)).astype(BF16)


def spread_mix(mix, high_ref, low_ref):
    row = lax.broadcasted_iota(jnp.int32, (MIX, HEADS), 0) // SLAB
    col = lax.broadcasted_iota(jnp.int32, (MIX, HEADS), 1)
    pick = jnp.where(row == col, 1.0, 0.0).astype(BF16)
    same = (lax.broadcasted_iota(jnp.int32, (MIX, MIX), 0) % SLAB) == (
        lax.broadcasted_iota(jnp.int32, (MIX, MIX), 1) % SLAB
    )
    for part, ref in zip(split(mix), (high_ref, low_ref)):
        tall = dot(pick, part).astype(BF16)
        full = lax.dot_general(tall, pick, (((1,), (1,)), ((), ())), preferred_element_type=F32)
        ref[...] = jnp.where(same, full, 0.0).astype(BF16)


def kernel(
    act, w_query, w_key, w_value, pre_mix, post_mix, span_place, out,
    act_v, w_v, res, stage, q_buf, k_buf, v_buf, scores, stat, stat_in, key_pos,
    part, part_in, pre_high, pre_low, post_high, post_low,
    act_sem, w_sem, own_sem, a2a_send, a2a_recv, y_send, y_recv, q_send, q_recv,
    stat_send, stat_recv, p_send, p_recv,
):
    ctx, tp = lax.axis_index("ctx"), lax.axis_index("tp")
    xh, y, core = ctx // 8, (ctx // 2) % 4, ctx % 2
    up = (xh * 8 + ((y + 1) % 4) * 2 + core, tp)
    down = (xh * 8 + ((y + 3) % 4) * 2 + core, tp)
    y_up, y_down = (y + 1) % 4, (y + 3) % 4
    sibling = (ctx + 1 - 2 * core, tp)
    partner = ((1 - xh) * 8 + y * 2 + core, tp)
    diagonal = ((1 - xh) * 8 + y * 2 + 1 - core, tp)
    mine = xh * 2 + core
    sibling_slot = xh * 2 + 1 - core
    partner_slot = (1 - xh) * 2 + core
    diagonal_slot = (1 - xh) * 2 + 1 - core
    peers = [(ctx, (tp + o) % SEQS) for o in range(1, SEQS)]

    weights = (w_query, w_key, w_value)
    buffers = (q_buf, k_buf, v_buf)

    act_copies = []
    for b in range(3):
        rows = pl.ds(b * 32, 32)
        act_copies.append(pltpu.make_async_copy(act.at[rows], act_v.at[rows], act_sem.at[b]))
    w_copies = []
    for n, (kind, j) in enumerate(CHUNKS):
        w_copies.append(
            pltpu.make_async_copy(weights[kind].at[:, pl.ds(j * WIDE, WIDE)], w_v.at[n], w_sem.at[n])
        )
    w_copies[0].start()
    for c in act_copies:
        c.start()

    barrier = pltpu.get_barrier_semaphore()
    friends = peers + [up, down, sibling, partner, diagonal]
    for friend in friends:
        pl.semaphore_signal(barrier, inc=1, device_id=friend, device_id_type=MESH)

    spread_mix(pre_mix[...] * (HD ** -0.5), pre_high, pre_low)
    spread_mix(post_mix[...], post_high, post_low)
    stat[...] = jnp.zeros_like(stat)
    column = lax.broadcasted_iota(jnp.int32, (SLAB, TILE), 1)
    position = column % SPAN
    for n in range(TILE // SPAN):
        place = span_place[(xh * 8 + (n // 2) * 2 + core) * 2 + n % 2]
        position = jnp.where(column // SPAN == n, position + place * SPAN, position)
    key_pos[...] = position

    sends = []

    def remote(src, dst, send, recv, to):
        copy = pltpu.make_async_remote_copy(
            src_ref=src, dst_ref=dst, send_sem=send, recv_sem=recv, device_id=to, device_id_type=MESH
        )
        sends.append(copy)
        return copy

    def slot_of(kind):
        return mine if kind == 0 else y

    exchange = {}

    def project(n):
        kind, j = CHUNKS[n]
        w_copies[n].wait()
        for b in range(3):
            if n == 0:
                act_copies[b].wait()
                if b == 2:
                    w_copies[1].start()
                    w_copies[2].start()
            rows = act_v[b * 32:(b + 1) * 32].reshape(32 * SEQS, MODEL)
            both = dot(rows, w_v[n])
            for i in range(2):
                res[i] = both[:, i * HD:(i + 1) * HD]
            for s in range(SEQS):
                for i in range(2):
                    stage[n, s, b * 32:(b + 1) * 32, i * HD:(i + 1) * HD] = res[
                        i, pl.ds(s, 32, stride=SEQS), :
                    ].astype(BF16)
        if n == 0:
            pl.semaphore_wait(barrier, len(friends))
        elif n + 2 < len(CHUNKS):
            w_copies[n + 2].start()
        here = buffers[kind].at[j, slot_of(kind), :, pl.ds(pl.multiple_of(tp * WIDE, WIDE), WIDE)]
        copies = []
        for o, peer in enumerate(peers):
            copies.append(
                remote(stage.at[n, peer[1]], here, a2a_send.at[n, o], a2a_recv.at[n, o], peer)
            )
            copies[-1].start()
        own = pltpu.make_async_copy(stage.at[n, tp], here, own_sem.at[n])
        own.start()
        exchange[n] = (copies, own)

    def arrived(n):
        copies, own = exchange[n]
        own.wait()
        for c in copies:
            c.wait_recv()

    ring = {}

    def ring_start(n, r):
        kind, j = CHUNKS[n]
        buf = buffers[kind]
        arrived(n)
        a = remote(buf.at[j, y], buf.at[j, y], y_send.at[r, 0], y_recv.at[r, 0], up)
        b = remote(buf.at[j, y], buf.at[j, y], y_send.at[r, 1], y_recv.at[r, 1], down)
        a.start()
        b.start()
        ring[r] = [a, b]

    def ring_forward(n, r):
        kind, j = CHUNKS[n]
        buf = buffers[kind]
        a, b = ring[r]
        a.wait_recv()
        first = buf.at[j, y_down, pl.ds(0, 48)]
        c = remote(first, first, y_send.at[r, 2], y_recv.at[r, 2], up)
        c.start()
        b.wait_recv()
        second = buf.at[j, y_up, pl.ds(48, 48)]
        d = remote(second, second, y_send.at[r, 3], y_recv.at[r, 3], down)
        d.start()
        ring[r] = [c, d]

    def ring_finish(r):
        for c in ring[r]:
            c.wait_recv()

    queries = {}

    def query_start(n):
        _, j = CHUNKS[n]
        arrived(n)
        a = remote(q_buf.at[j, mine], q_buf.at[j, mine], q_send.at[j, 1], q_recv.at[j, 1], partner)
        b = remote(q_buf.at[j, mine], q_buf.at[j, mine], q_send.at[j, 0], q_recv.at[j, 0], sibling)
        a.start()
        b.start()
        queries[j] = [a, b]

    def query_forward(j):
        a, b = queries[j]
        a.wait_recv()
        there = q_buf.at[j, partner_slot]
        c = remote(there, there, q_send.at[j, 2], q_recv.at[j, 2], sibling)
        c.start()
        queries[j] = [b, c]

    def query_finish(j):
        for c in queries[j]:
            c.wait_recv()

    def score(j):
        def one(g, carry):
            for u in range(4):
                hh = g * 4 + u
                lanes = pl.ds(pl.multiple_of(hh * HD, HD), HD)
                q = q_buf[j, :, :, lanes].reshape(TILE, HD)
                k = k_buf[j, :, :, lanes].reshape(TILE, HD)
                scores[(hh // 2) * 4 + 2 * j + hh % 2] = lax.dot_general(
                    q, k, (((1,), (1,)), ((), ())), preferred_element_type=F32
                )
            return carry

        lax.fori_loop(0, HEADS // 8, one, 0)

    lane = lax.broadcasted_iota(jnp.int32, (MIX, 128), 1)
    minor = lax.broadcasted_iota(jnp.int32, (SLAB, 1), 0)
    half = (1 - xh, xh)
    GROUP = SLABS // 2

    def softmax(group):
        def one(g, carry):
            slabs = [g * 4 + u for u in range(4)]
            rows = [
                pl.ds(pl.multiple_of((half[group] * GROUP + i) * SLAB, SLAB), SLAB) for i in slabs
            ]
            x = jnp.concatenate([scores[:, r, :].reshape(MIX, TILE) for r in rows], axis=1)
            high, low = split(x)
            logits = dot(pre_high[...], high) + dot(pre_low[...], high) + dot(pre_high[...], low)
            stats = stat[group]
            for u, (i, r) in enumerate(zip(slabs, rows)):
                span = i // 6
                place = span_place[((half[group] * 8 + y * 2) + span // 2) * 2 + span % 2]
                seen = key_pos[...] <= place * SPAN + (i % 6) * SLAB + minor
                mine_logits = logits[:, u * TILE:(u + 1) * TILE].reshape(HEADS, SLAB, TILE)
                masked = jnp.where(seen[None], mine_logits, FLOOR).reshape(MIX, TILE)
                top = jnp.max(masked, axis=1, keepdims=True)
                e = jnp.exp(masked - top)
                total = jnp.sum(e, axis=1, keepdims=True)
                scores[:, r, :] = e.reshape(HEADS, SLAB, TILE)
                stats = jnp.where(lane == i, top, jnp.where(lane == i + 64, total, stats))
            stat[group] = stats
            return carry

        lax.fori_loop(0, GROUP // 4, one, 0)

    stat_copies = {}

    def stat_start(group):
        copies = []
        for n, to in enumerate((sibling, partner, diagonal)):
            copies.append(
                remote(
                    stat.at[group], stat_in.at[half[group], n],
                    stat_send.at[group, n], stat_recv.at[half[group], n], to,
                )
            )
            copies[-1].start()
        stat_copies[group] = copies

    def stat_finish(group):
        for c in stat_copies[group]:
            c.wait_recv()
        for c in stat_copies[group]:
            c.wait_send()
        for c in stat_copies[group]:
            sends[:] = [d for d in sends if d is not c]
        own = stat[group]
        others = [stat_in[half[group], n] for n in range(3)]
        top = functools.reduce(jnp.maximum, others, own)
        total = sum(jnp.exp(s - top) * pltpu.roll(s, 64, 1) for s in [own] + others)
        stat[group] = jnp.exp(own - top) / total

    def post(group):
        def one(g, carry):
            slabs = [g * 6 + u for u in range(6)]
            rows = [
                pl.ds(pl.multiple_of((half[group] * GROUP + i) * SLAB, SLAB), SLAB) for i in slabs
            ]
            weights = stat[group]
            probs = []
            for i, r in zip(slabs, rows):
                weight = jnp.sum(jnp.where(lane == i, weights, 0.0), axis=1, keepdims=True)
                probs.append((scores[:, r, :].reshape(MIX, TILE) * weight).astype(BF16))
            probs = jnp.concatenate(probs, axis=1)
            mixed = dot(post_high[...], probs) + dot(post_low[...], probs)
            for u, r in enumerate(rows):
                scores[:, r, :] = mixed[:, u * TILE:(u + 1) * TILE].reshape(HEADS, SLAB, TILE)
            return carry

        lax.fori_loop(0, GROUP // 6, one, 0)

    def attend(j, group):
        rows = pl.ds(pl.multiple_of(half[group] * 2 * ROWS, 2 * ROWS), 2 * ROWS)
        slots = pl.ds(half[group] * 2, 2)

        def one(g, carry):
            for u in range(4):
                hh = g * 4 + u
                lanes = pl.ds(pl.multiple_of(hh * HD, HD), HD)
                v = v_buf[j, :, :, lanes].reshape(TILE, HD)
                m = scores[(hh // 2) * 4 + 2 * j + hh % 2, rows, :].astype(BF16)
                part[j, slots, :, lanes] = dot(m, v).reshape(2, ROWS, HD).astype(BF16)
            return carry

        lax.fori_loop(0, HEADS // 8, one, 0)

    partial = {}

    def partial_start(j, group):
        slot = (diagonal_slot, sibling_slot)[group]
        a = remote(
            part.at[j, slot], part_in.at[j, group], p_send.at[j, group], p_recv.at[j, group], sibling
        )
        a.start()
        partial[j, group] = a

    def partial_cross(j):
        partial[j, 0].wait_recv()
        part[j, partner_slot] = (
            part[j, partner_slot].astype(F32) + part_in[j, 0].astype(F32)
        ).astype(BF16)
        c = remote(part.at[j, partner_slot], part_in.at[j, 2], p_send.at[j, 2], p_recv.at[j, 2], partner)
        c.start()
        partial[j, 2] = c

    def partial_finish(j):
        partial[j, 1].wait_recv()
        partial[j, 2].wait_recv()
        done = (
            part[j, mine].astype(F32) + part_in[j, 1].astype(F32) + part_in[j, 2].astype(F32)
        ).astype(BF16)
        for t in range(SEQS):
            out[:, t * 2 * WIDE + j * WIDE:t * 2 * WIDE + (j + 1) * WIDE] = done[:, t * WIDE:(t + 1) * WIDE]

    project(0)
    project(1)
    project(2)
    ring_start(0, 0)
    project(3)
    project(4)
    query_start(1)
    project(5)
    ring_start(2, 1)
    ring_forward(0, 0)
    query_start(3)
    query_forward(0)
    ring_start(4, 2)
    ring_finish(0)
    query_finish(0)
    score(0)
    ring_forward(2, 1)
    query_forward(1)
    ring_start(5, 3)
    ring_finish(1)
    query_finish(1)
    score(1)
    softmax(0)
    stat_start(0)
    ring_forward(4, 2)
    softmax(1)
    stat_start(1)
    stat_finish(0)
    post(0)
    ring_forward(5, 3)
    ring_finish(2)
    attend(0, 0)
    partial_start(0, 0)
    stat_finish(1)
    post(1)
    partial_cross(0)
    attend(0, 1)
    partial_start(0, 1)
    ring_finish(3)
    attend(1, 0)
    partial_start(1, 0)
    attend(1, 1)
    partial_cross(1)
    partial_start(1, 1)
    partial_finish(0)
    partial_finish(1)
    for c in sends:
        c.wait_send()


def local(activations, w_query, w_key, w_value, pre_mix, post_mix, span_place):
    any_spec = pl.BlockSpec(memory_space=pl.ANY)
    vmem = pl.BlockSpec(memory_space=pltpu.VMEM)
    dma = pltpu.SemaphoreType.DMA
    out = pl.pallas_call(
        kernel,
        name="heads",
        out_shape=jax.ShapeDtypeStruct((ROWS, MODEL), BF16),
        in_specs=[any_spec] * 4 + [vmem] * 2 + [pl.BlockSpec(memory_space=pltpu.SMEM)],
        out_specs=vmem,
        scratch_shapes=[
            pltpu.VMEM((ROWS, SEQS, MODEL), BF16),
            pltpu.VMEM((6, MODEL, WIDE), BF16),
            pltpu.VMEM((2, 256, HD), F32),
            pltpu.VMEM((6, SEQS, ROWS, WIDE), BF16),
            pltpu.VMEM((2, 4, ROWS, HALF), BF16),
            pltpu.VMEM((2, 4, ROWS, HALF), BF16),
            pltpu.VMEM((2, 4, ROWS, HALF), BF16),
            pltpu.VMEM((HEADS, TILE, TILE), F32),
            pltpu.VMEM((2, MIX, 128), F32),
            pltpu.VMEM((2, 3, MIX, 128), F32),
            pltpu.VMEM((SLAB, TILE), jnp.int32),
            pltpu.VMEM((2, 4, ROWS, HALF), BF16),
            pltpu.VMEM((2, 3, ROWS, HALF), BF16),
            pltpu.VMEM((MIX, MIX), BF16),
            pltpu.VMEM((MIX, MIX), BF16),
            pltpu.VMEM((MIX, MIX), BF16),
            pltpu.VMEM((MIX, MIX), BF16),
            dma((3,)), dma((6,)), dma((6,)),
            dma((6, 7)), dma((6, 7)),
            dma((4, 4)), dma((4, 4)),
            dma((2, 3)), dma((2, 3)),
            dma((2, 3)), dma((2, 3)),
            dma((2, 3)), dma((2, 3)),
        ],
        compiler_params=pltpu.CompilerParams(
            collective_id=0, has_side_effects=True, vmem_limit_bytes=60 * 2**20
        ),
        cost_estimate=pl.CostEstimate(flops=30 * 10**9, bytes_accessed=30 * 10**6, transcendentals=5 * 10**6),
    )(activations, w_query, w_key, w_value, pre_mix, post_mix, span_place)
    return out.reshape(ROWS, 1, MODEL)


def solution(mesh):
    placed = (P("ctx", None, None), P(None, "tp"), P(None, "tp"), P(None, "tp"), P(), P(), P())
    return jax.shard_map(
        local, mesh=mesh, in_specs=placed, out_specs=P("ctx", "tp", None), check_vma=False
    )
```

```python
import functools

import jax
import jax.numpy as jnp
from jax import lax
from jax.experimental import pallas as pl
from jax.experimental.pallas import tpu as pltpu
from jax.sharding import PartitionSpec as P

HEADS = 32
HD = 128
SPAN = 48
MODEL = 4096
SEQS = 8
ROWS = 96
TILE = 384
SLAB = 8
SLABS = TILE // SLAB
MIX = HEADS * SLAB
WIDE = 256
PARTS = 4
PART = MODEL // PARTS
FLOOR = -1e30
GROUPS = 3
GROUP_ROWS = ROWS // GROUPS
GROUP_SLABS = SLABS // GROUPS
MESH = pl.DeviceIdType.MESH
F32 = jnp.float32
BF16 = jnp.bfloat16

QUERY, KEY, VALUE = 0, 1, 2

CHUNKS = ((KEY, 0), (KEY, 1), (QUERY, 0), (QUERY, 1), (VALUE, 0), (VALUE, 1))

MOVES = (
    (KEY, 0, 0, 32), (KEY, 0, 32, 32), (KEY, 0, 64, 32), (KEY, 1, 0, 96),
    (VALUE, 0, 0, 96), (VALUE, 1, 0, 96), (VALUE, 2, 0, 96), (VALUE, 3, 0, 96),
    (QUERY, 0, 0, 96), (QUERY, 1, 0, 96),
)


def dot(a, b):
    return jnp.dot(a, b, preferred_element_type=F32)


def split(x):
    high = x.astype(BF16)
    return high, (x - high.astype(F32)).astype(BF16)


def spread_mix(mix, high_ref, low_ref):
    row = lax.broadcasted_iota(jnp.int32, (MIX, HEADS), 0) // SLAB
    col = lax.broadcasted_iota(jnp.int32, (MIX, HEADS), 1)
    pick = jnp.where(row == col, 1.0, 0.0).astype(BF16)
    same = (lax.broadcasted_iota(jnp.int32, (MIX, MIX), 0) % SLAB) == (
        lax.broadcasted_iota(jnp.int32, (MIX, MIX), 1) % SLAB
    )
    for part, ref in zip(split(mix), (high_ref, low_ref)):
        tall = dot(pick, part).astype(BF16)
        full = lax.dot_general(tall, pick, (((1,), (1,)), ((), ())), preferred_element_type=F32)
        ref[...] = jnp.where(same, full, 0.0).astype(BF16)


def kernel(
    act, w_query, w_key, w_value, pre_mix, post_mix, span_place, out,
    act_v, w_v, res, stage, stage_v, q_buf, k_buf, v_buf, scores, stat, stat_out, stat_in, key_pos, logits_even, logits_odd,
    part, part_in, pre_high, pre_low, post_high, post_low,
    act_sem, w_sem, own_sem, a2a_send, a2a_recv, y_send, y_recv, q_send, q_recv,
    stat_send, stat_recv, p_send, p_recv,
):
    ctx, tp = lax.axis_index("ctx"), lax.axis_index("tp")
    xh, y, core = ctx // 8, (ctx // 2) % 4, ctx % 2
    up = (xh * 8 + ((y + 1) % 4) * 2 + core, tp)
    down = (xh * 8 + ((y + 3) % 4) * 2 + core, tp)
    y_up, y_down = (y + 1) % 4, (y + 3) % 4
    sibling = (ctx + 1 - 2 * core, tp)
    partner = ((1 - xh) * 8 + y * 2 + core, tp)
    diagonal = ((1 - xh) * 8 + y * 2 + 1 - core, tp)
    mine = xh * 2 + core
    sibling_slot = xh * 2 + 1 - core
    partner_slot = (1 - xh) * 2 + core
    diagonal_slot = (1 - xh) * 2 + 1 - core
    peers = [(ctx, (tp + o) % SEQS) for o in range(1, SEQS)]

    weights = (w_query, w_key, w_value)
    buffers = (q_buf, k_buf, v_buf)

    act_copies = []
    for b in range(3):
        rows = pl.ds(b * 32, 32)
        act_copies.append(pltpu.make_async_copy(act.at[rows], act_v.at[rows], act_sem.at[b]))
    w_copies = []
    for n, (kind, j) in enumerate(CHUNKS):
        w_copies.append(
            pltpu.make_async_copy(weights[kind].at[:, pl.ds(j * WIDE, WIDE)], w_v.at[n % 3], w_sem.at[n])
        )
    w_copies[0].start()
    for c in act_copies:
        c.start()

    barrier = pltpu.get_barrier_semaphore()
    friends = peers + [up, down, sibling, partner, diagonal]
    for friend in friends:
        pl.semaphore_signal(barrier, inc=1, device_id=friend, device_id_type=MESH)

    spread_mix(pre_mix[...] * (HD ** -0.5), pre_high, pre_low)
    spread_mix(post_mix[...], post_high, post_low)
    stat[...] = jnp.zeros_like(stat)
    column = lax.broadcasted_iota(jnp.int32, (SLAB, TILE), 1)
    position = column % SPAN
    for n in range(TILE // SPAN):
        place = span_place[(xh * 8 + (n // 2) * 2 + core) * 2 + n % 2]
        position = jnp.where(column // SPAN == n, position + place * SPAN, position)
    key_pos[...] = position

    sends = []

    def remote(src, dst, send, recv, to):
        copy = pltpu.make_async_remote_copy(
            src_ref=src, dst_ref=dst, send_sem=send, recv_sem=recv, device_id=to, device_id_type=MESH
        )
        sends.append(copy)
        return copy

    def slot_of(kind):
        return mine if kind == 0 else y

    exchange = {}

    def project(n):
        kind, j = CHUNKS[n]
        w_copies[n].wait()
        for b in range(3):
            if n == 0:
                act_copies[b].wait()
                if b == 2:
                    w_copies[1].start()
                    w_copies[2].start()
            rows = act_v[b * 32:(b + 1) * 32].reshape(32 * SEQS, MODEL)
            both = dot(rows, w_v[n % 3])
            for i in range(2):
                res[i] = both[:, i * HD:(i + 1) * HD]
            for s in range(SEQS):
                for i in range(2):
                    block = res[i, pl.ds(s, 32, stride=SEQS), :].astype(BF16)
                    if kind == VALUE:
                        stage_v[2 * j + i, s, b * 32:(b + 1) * 32, :] = block
                    else:
                        stage[kind, j, s, b * 32:(b + 1) * 32, i * HD:(i + 1) * HD] = block
            if n == 0:
                if b == 0:
                    pl.semaphore_wait(barrier, len(friends))
                scatter(b)
        if n > 0 and n + 2 < len(CHUNKS):
            w_copies[n + 2].start()

    def scatter(e):
        kind, j, row, rows = MOVES[e]
        source, width = (stage_v.at[j], HD) if kind == VALUE else (stage.at[kind, j], WIDE)
        rows = pl.ds(row, rows)
        here = buffers[kind].at[j, slot_of(kind), rows, pl.ds(pl.multiple_of(tp * width, width), width)]
        copies = []
        for o, peer in enumerate(peers):
            copies.append(
                remote(source.at[peer[1], rows], here, a2a_send.at[e, o], a2a_recv.at[e, o], peer)
            )
            copies[-1].start()
        own = pltpu.make_async_copy(source.at[tp, rows], here, own_sem.at[e])
        own.start()
        exchange[e] = (copies, own)

    def arrived(e):
        copies, own = exchange[e]
        own.wait()
        for c in copies:
            c.wait_recv()

    ring = {}

    def ring_start(e):
        kind, j, row, rows = MOVES[e]
        arrived(e)
        block = buffers[kind].at[j, y, pl.ds(row, rows)]
        copies = []
        for m, to in enumerate((up, down)):
            copies.append(remote(block, block, y_send.at[e, m], y_recv.at[e, m], to))
            copies[-1].start()
        ring[e] = copies

    def ring_forward(e):
        kind, j, row, rows = MOVES[e]
        copies = ring[e]
        for m, (source, to) in enumerate(((y_down, up), (y_up, down))):
            copies[m].wait_recv()
            block = buffers[kind].at[j, source, pl.ds(row + m * (rows // 2), rows // 2)]
            copies[m] = remote(block, block, y_send.at[e, 2 + m], y_recv.at[e, 2 + m], to)
            copies[m].start()

    def ring_finish(e):
        for c in ring[e]:
            c.wait_recv()

    queries = {}

    def query_start(j):
        arrived(8 + j)
        a = remote(q_buf.at[j, mine], q_buf.at[j, mine], q_send.at[j, 1], q_recv.at[j, 1], partner)
        b = remote(q_buf.at[j, mine], q_buf.at[j, mine], q_send.at[j, 0], q_recv.at[j, 0], sibling)
        a.start()
        b.start()
        queries[j] = [a, b]

    def query_forward(j):
        a, b = queries[j]
        a.wait_recv()
        there = q_buf.at[j, partner_slot]
        c = remote(there, there, q_send.at[j, 2], q_recv.at[j, 2], sibling)
        c.start()
        queries[j] = [b, c]

    def query_finish(j):
        for c in queries[j]:
            c.wait_recv()

    def score(j):
        def one(g, carry):
            for u in range(4):
                hh = g * 4 + u
                lanes = pl.ds(pl.multiple_of(hh * HD, HD), HD)
                q = q_buf[j, :, :, lanes].reshape(TILE, HD)
                k = k_buf[j, :, :, lanes].reshape(TILE, HD)
                scores[(hh // 2) * PARTS + 2 * j + hh % 2] = lax.dot_general(
                    q, k, (((1,), (1,)), ((), ())), preferred_element_type=F32
                )
            return carry

        lax.fori_loop(0, HEADS // 8, one, 0)

    lane = lax.broadcasted_iota(jnp.int32, (MIX, 128), 1)
    minor = lax.broadcasted_iota(jnp.int32, (SLAB, 1), 0)
    per_slot = GROUP_ROWS // SLAB

    logits_of = (logits_even, logits_odd)

    def slab_rows(step, u):
        group, slot = divmod(step, 4)
        first = slot * ROWS + group * GROUP_ROWS + u * SLAB
        return slice(first, first + SLAB)

    def premix(step):
        x = jnp.concatenate(
            [scores[:, slab_rows(step, u), :].reshape(MIX, TILE) for u in range(per_slot)], axis=1
        )
        high, low = split(x)
        logits_of[step % 2][...] = dot(pre_high[...], high) + dot(pre_low[...], high) + dot(pre_high[...], low)

    def softmax_step(step):
        group, slot = divmod(step, 4)
        stats = stat[group]
        for u in range(per_slot):
            i = slot * per_slot + u
            inside = group * GROUP_ROWS + u * SLAB
            span = ((slot // 2) * 8 + y * 2 + slot % 2) * 2 + inside // SPAN
            seen = key_pos[...] <= span_place[span] * SPAN + inside % SPAN + minor
            logits = logits_of[step % 2][:, u * TILE:(u + 1) * TILE].reshape(HEADS, SLAB, TILE)
            masked = jnp.where(seen[None], logits, FLOOR).reshape(MIX, TILE)
            top = jnp.max(masked, axis=1, keepdims=True)
            e = jnp.exp(masked - top)
            total = jnp.sum(e, axis=1, keepdims=True)
            scores[:, slab_rows(step, u), :] = e.reshape(HEADS, SLAB, TILE)
            stats = jnp.where(lane == i, top, jnp.where(lane == i + GROUP_SLABS, total, stats))
        stat[group] = stats

    def softmax(first, last):
        if first == 0:
            premix(0)
        for step in range(first, last):
            if step + 1 < 4 * GROUPS:
                premix(step + 1)
            softmax_step(step)

    stat_copies = {}

    def stat_start(group):
        packed = stat[group, 0:64, :]
        for q in range(1, 4):
            packed += pltpu.roll(stat[group, q * 64:(q + 1) * 64, :], q * 32, 1)
        stat_out[group] = packed
        copies = []
        for n, to in enumerate((sibling, partner, diagonal)):
            copies.append(
                remote(
                    stat_out.at[group], stat_in.at[group, n],
                    stat_send.at[group, n], stat_recv.at[group, n], to,
                )
            )
            copies[-1].start()
        stat_copies[group] = copies

    def stat_finish(group):
        for c in stat_copies[group]:
            c.wait_recv()
        own = stat_out[group]
        others = [stat_in[group, n] for n in range(3)]
        top = functools.reduce(jnp.maximum, others, own)
        total = sum(jnp.exp(s - top) * pltpu.roll(s, 128 - GROUP_SLABS, 1) for s in [own] + others)
        weights = jnp.exp(own - top) / total
        stat[group, 0:64, :] = weights
        for q in range(1, 4):
            stat[group, q * 64:(q + 1) * 64, :] = pltpu.roll(weights, 128 - q * 32, 1)

    far, near = 1 - xh, xh

    def post(group, pair):
        slabs = [pair * 2 * per_slot + u for u in range(2 * per_slot)]
        rows = [
            pl.ds(
                pl.multiple_of(
                    (pair * 2 + u // per_slot) * ROWS + group * GROUP_ROWS + (u % per_slot) * SLAB, SLAB
                ),
                SLAB,
            )
            for u in range(2 * per_slot)
        ]
        weights = stat[group]
        probs = []
        for i, r in zip(slabs, rows):
            weight = jnp.sum(jnp.where(lane == i, weights, 0.0), axis=1, keepdims=True)
            probs.append((scores[:, r, :].reshape(MIX, TILE) * weight).astype(BF16))
        probs = jnp.concatenate(probs, axis=1)
        mixed = dot(post_high[...], probs) + dot(post_low[...], probs)
        for u, r in enumerate(rows):
            scores[:, r, :] = mixed[:, u * TILE:(u + 1) * TILE].reshape(HEADS, SLAB, TILE)

    def attend(j, pair):
        rows = pl.ds(pl.multiple_of(pair * 2 * ROWS, 2 * ROWS), 2 * ROWS)

        def one(g, carry):
            for u in range(4):
                t = g * 4 + u
                lanes = pl.ds(pl.multiple_of(t * HD, HD), HD)
                v = v_buf[j, :, :, lanes].reshape(TILE, HD)
                m = scores[t * PARTS + j, rows, :].astype(BF16)
                part[j, pl.ds(pair * 2, 2), :, lanes] = dot(m, v).reshape(2, ROWS, HD).astype(BF16)
            return carry

        lax.fori_loop(0, SEQS // 4, one, 0)

    partial = {}

    def partial_start(j, n):
        slot = (diagonal_slot, sibling_slot)[n]
        partial[j, n] = remote(part.at[j, slot], part_in.at[j, n], p_send.at[j, n], p_recv.at[j, n], sibling)
        partial[j, n].start()

    def attend_far(j):
        attend(j, far)
        partial_start(j, 0)

    def attend_near(j):
        attend(j, near)
        partial_start(j, 1)

    def partial_cross(j):
        partial[j, 0].wait_recv()
        both = part.at[j, partner_slot]
        both[...] = (both[...].astype(F32) + part_in[j, 0].astype(F32)).astype(BF16)
        partial[j, 2] = remote(both, part_in.at[j, 2], p_send.at[j, 2], p_recv.at[j, 2], partner)
        partial[j, 2].start()

    def partial_finish(j):
        partial[j, 1].wait_recv()
        partial[j, 2].wait_recv()
        done = (
            part[j, mine].astype(F32) + part_in[j, 1].astype(F32) + part_in[j, 2].astype(F32)
        ).astype(BF16)
        for t in range(SEQS):
            head = t * PARTS + j
            out[:, head * HD:(head + 1) * HD] = done[:, t * HD:(t + 1) * HD]

    project(0)
    project(1)
    ring_start(0)
    scatter(3)
    project(2)
    scatter(8)
    ring_start(1)
    ring_start(2)
    project(3)
    scatter(9)
    ring_forward(0)
    ring_forward(1)
    project(4)
    ring_start(3)
    ring_forward(2)
    scatter(4)
    scatter(5)
    project(5)
    scatter(6)
    scatter(7)
    query_start(0)
    query_start(1)
    ring_forward(3)
    ring_start(4)
    query_forward(0)
    ring_start(5)
    ring_finish(0)
    ring_finish(1)
    ring_finish(2)
    query_finish(0)
    score(0)
    query_forward(1)
    ring_finish(3)
    query_finish(1)
    score(1)
    softmax(0, 2)
    ring_start(6)
    ring_start(7)
    softmax(2, 4)
    stat_start(0)
    ring_forward(4)
    softmax(4, 8)
    stat_start(1)
    ring_forward(5)
    softmax(8, 12)
    stat_start(2)
    stat_finish(0)
    post(0, far)
    stat_finish(1)
    post(1, far)
    ring_forward(6)
    stat_finish(2)
    post(2, far)
    ring_finish(4)
    attend_far(0)
    ring_finish(5)
    attend_far(1)
    partial_cross(0)
    ring_forward(7)
    post(0, near)
    partial_cross(1)
    ring_finish(6)
    attend_far(2)
    post(1, near)
    partial_cross(2)
    post(2, near)
    ring_finish(7)
    attend_far(3)
    attend_near(0)
    partial_cross(3)
    attend_near(1)
    attend_near(2)
    attend_near(3)
    partial_finish(0)
    partial_finish(1)
    partial_finish(2)
    partial_finish(3)
    for c in sends:
        c.wait_send()


def local(activations, w_query, w_key, w_value, pre_mix, post_mix, span_place):
    any_spec = pl.BlockSpec(memory_space=pl.ANY)
    vmem = pl.BlockSpec(memory_space=pltpu.VMEM)
    dma = pltpu.SemaphoreType.DMA
    out = pl.pallas_call(
        kernel,
        name="heads",
        out_shape=jax.ShapeDtypeStruct((ROWS, MODEL), BF16),
        in_specs=[any_spec] * 4 + [vmem] * 2 + [pl.BlockSpec(memory_space=pltpu.SMEM)],
        out_specs=vmem,
        scratch_shapes=[
            pltpu.VMEM((ROWS, SEQS, MODEL), BF16),
            pltpu.VMEM((3, MODEL, WIDE), BF16),
            pltpu.VMEM((2, 256, HD), F32),
            pltpu.VMEM((2, 2, SEQS, ROWS, WIDE), BF16),
            pltpu.VMEM((PARTS, SEQS, ROWS, HD), BF16),
            pltpu.VMEM((2, 4, ROWS, 2 * PART), BF16),
            pltpu.VMEM((2, 4, ROWS, 2 * PART), BF16),
            pltpu.VMEM((PARTS, 4, ROWS, PART), BF16),
            pltpu.VMEM((HEADS, TILE, TILE), F32),
            pltpu.VMEM((GROUPS, MIX, 128), F32),
            pltpu.VMEM((GROUPS, MIX // 4, 128), F32),
            pltpu.VMEM((GROUPS, 3, MIX // 4, 128), F32),
            pltpu.VMEM((SLAB, TILE), jnp.int32),
            pltpu.VMEM((MIX, GROUP_SLABS // 4 * TILE), F32),
            pltpu.VMEM((MIX, GROUP_SLABS // 4 * TILE), F32),
            pltpu.VMEM((PARTS, 4, ROWS, PART), BF16),
            pltpu.VMEM((PARTS, 3, ROWS, PART), BF16),
            pltpu.VMEM((MIX, MIX), BF16),
            pltpu.VMEM((MIX, MIX), BF16),
            pltpu.VMEM((MIX, MIX), BF16),
            pltpu.VMEM((MIX, MIX), BF16),
            dma((3,)), dma((len(CHUNKS),)), dma((len(MOVES),)),
            dma((len(MOVES), SEQS - 1)), dma((len(MOVES), SEQS - 1)),
            dma((len(MOVES) - 2, 4)), dma((len(MOVES) - 2, 4)),
            dma((2, 3)), dma((2, 3)),
            dma((GROUPS, 3)), dma((GROUPS, 3)),
            dma((PARTS, 3)), dma((PARTS, 3)),
        ],
        compiler_params=pltpu.CompilerParams(
            collective_id=0, has_side_effects=True, vmem_limit_bytes=60 * 2**20
        ),
        cost_estimate=pl.CostEstimate(flops=30 * 10**9, bytes_accessed=30 * 10**6, transcendentals=5 * 10**6),
    )(activations, w_query, w_key, w_value, pre_mix, post_mix, span_place)
    return out.reshape(ROWS, 1, MODEL)


def solution(mesh):
    placed = (P("ctx", None, None), P(None, "tp"), P(None, "tp"), P(None, "tp"), P(), P(), P())
    return jax.shard_map(
        local, mesh=mesh, in_specs=placed, out_specs=P("ctx", "tp", None), check_vma=False
    )
```

```python
import functools

import jax
import jax.numpy as jnp
from jax import lax
from jax.experimental import pallas as pl
from jax.experimental.pallas import tpu as pltpu
from jax.sharding import PartitionSpec as P

HEADS = 32
HD = 128
SPAN = 48
MODEL = 4096
SEQS = 8
ROWS = 96
TILE = 384
SLAB = 8
SLABS = TILE // SLAB
MIX = HEADS * SLAB
WIDE = 256
PARTS = 4
PART = MODEL // PARTS
FLOOR = -1e30
GROUPS = 3
GROUP_ROWS = ROWS // GROUPS
GROUP_SLABS = SLABS // GROUPS
MESH = pl.DeviceIdType.MESH
F32 = jnp.float32
BF16 = jnp.bfloat16

QUERY, KEY, VALUE = 0, 1, 2

CHUNKS = ((KEY, 0), (QUERY, 0), (KEY, 1), (QUERY, 1), (VALUE, 0), (VALUE, 1))

MOVES = (
    (KEY, 0, 0, 32), (KEY, 0, 32, 32), (KEY, 0, 64, 32), (KEY, 1, 0, 96),
    (VALUE, 0, 0, 96), (VALUE, 1, 0, 96), (VALUE, 2, 0, 96), (VALUE, 3, 0, 96),
    (QUERY, 0, 0, 96), (QUERY, 1, 0, 96),
)


def dot(a, b):
    return jnp.dot(a, b, preferred_element_type=F32)


def split(x):
    high = x.astype(BF16)
    return high, (x - high.astype(F32)).astype(BF16)


def spread_mix(mix, high_ref, low_ref):
    row = lax.broadcasted_iota(jnp.int32, (MIX, HEADS), 0) // SLAB
    col = lax.broadcasted_iota(jnp.int32, (MIX, HEADS), 1)
    pick = jnp.where(row == col, 1.0, 0.0).astype(BF16)
    same = (lax.broadcasted_iota(jnp.int32, (MIX, MIX), 0) % SLAB) == (
        lax.broadcasted_iota(jnp.int32, (MIX, MIX), 1) % SLAB
    )
    for part, ref in zip(split(mix), (high_ref, low_ref)):
        tall = dot(pick, part).astype(BF16)
        full = lax.dot_general(tall, pick, (((1,), (1,)), ((), ())), preferred_element_type=F32)
        ref[...] = jnp.where(same, full, 0.0).astype(BF16)


def kernel(
    act, w_query, w_key, w_value, pre_mix, post_mix, span_place, out,
    act_v, w_v, res, stage, stage_v, q_buf, k_buf, v_buf, scores, stat, stat_out, stat_in, key_pos, logits_even, logits_odd,
    part, part_in, pre_high, pre_low, post_high, post_low,
    act_sem, w_sem, own_sem, a2a_send, a2a_recv, y_send, y_recv, q_send, q_recv,
    stat_send, stat_recv, p_send, p_recv,
):
    ctx, tp = lax.axis_index("ctx"), lax.axis_index("tp")
    xh, y, core = ctx // 8, (ctx // 2) % 4, ctx % 2
    up = (xh * 8 + ((y + 1) % 4) * 2 + core, tp)
    down = (xh * 8 + ((y + 3) % 4) * 2 + core, tp)
    y_up, y_down = (y + 1) % 4, (y + 3) % 4
    sibling = (ctx + 1 - 2 * core, tp)
    partner = ((1 - xh) * 8 + y * 2 + core, tp)
    diagonal = ((1 - xh) * 8 + y * 2 + 1 - core, tp)
    mine = xh * 2 + core
    sibling_slot = xh * 2 + 1 - core
    partner_slot = (1 - xh) * 2 + core
    diagonal_slot = (1 - xh) * 2 + 1 - core
    peers = [(ctx, (tp + o) % SEQS) for o in range(1, SEQS)]

    weights = (w_query, w_key, w_value)
    buffers = (q_buf, k_buf, v_buf)

    act_copies = []
    for b in range(3):
        rows = pl.ds(b * 32, 32)
        act_copies.append(pltpu.make_async_copy(act.at[rows], act_v.at[rows], act_sem.at[b]))
    w_copies = []
    for n, (kind, j) in enumerate(CHUNKS):
        w_copies.append(
            pltpu.make_async_copy(weights[kind].at[:, pl.ds(j * WIDE, WIDE)], w_v.at[n % 3], w_sem.at[n])
        )
    w_copies[0].start()
    for c in act_copies:
        c.start()

    barrier = pltpu.get_barrier_semaphore()
    friends = peers + [up, down, sibling, partner, diagonal]
    for friend in friends:
        pl.semaphore_signal(barrier, inc=1, device_id=friend, device_id_type=MESH)

    spread_mix(pre_mix[...] * (HD ** -0.5), pre_high, pre_low)
    spread_mix(post_mix[...], post_high, post_low)
    stat[...] = jnp.zeros_like(stat)
    column = lax.broadcasted_iota(jnp.int32, (SLAB, TILE), 1)
    position = column % SPAN
    for n in range(TILE // SPAN):
        place = span_place[(xh * 8 + (n // 2) * 2 + core) * 2 + n % 2]
        position = jnp.where(column // SPAN == n, position + place * SPAN, position)
    key_pos[...] = position

    sends = []

    def remote(src, dst, send, recv, to):
        copy = pltpu.make_async_remote_copy(
            src_ref=src, dst_ref=dst, send_sem=send, recv_sem=recv, device_id=to, device_id_type=MESH
        )
        sends.append(copy)
        return copy

    def slot_of(kind):
        return mine if kind == 0 else y

    exchange = {}

    def project(n):
        kind, j = CHUNKS[n]
        w_copies[n].wait()
        for b in range(3):
            if n == 0:
                act_copies[b].wait()
                if b == 2:
                    w_copies[1].start()
                    w_copies[2].start()
            rows = act_v[b * 32:(b + 1) * 32].reshape(32 * SEQS, MODEL)
            both = dot(rows, w_v[n % 3])
            for i in range(2):
                res[i] = both[:, i * HD:(i + 1) * HD]
            for s in range(SEQS):
                for i in range(2):
                    block = res[i, pl.ds(s, 32, stride=SEQS), :].astype(BF16)
                    if kind == VALUE:
                        stage_v[2 * j + i, s, b * 32:(b + 1) * 32, :] = block
                    else:
                        stage[kind, j, s, b * 32:(b + 1) * 32, i * HD:(i + 1) * HD] = block
            if n == 0:
                if b == 0:
                    pl.semaphore_wait(barrier, len(friends))
                scatter(b)
        if n > 0 and n + 2 < len(CHUNKS):
            w_copies[n + 2].start()

    def scatter(e):
        kind, j, row, rows = MOVES[e]
        source, width = (stage_v.at[j], HD) if kind == VALUE else (stage.at[kind, j], WIDE)
        rows = pl.ds(row, rows)
        here = buffers[kind].at[j, slot_of(kind), rows, pl.ds(pl.multiple_of(tp * width, width), width)]
        copies = []
        for o, peer in enumerate(peers):
            copies.append(
                remote(source.at[peer[1], rows], here, a2a_send.at[e, o], a2a_recv.at[e, o], peer)
            )
            copies[-1].start()
        own = pltpu.make_async_copy(source.at[tp, rows], here, own_sem.at[e])
        own.start()
        exchange[e] = (copies, own)

    def arrived(e):
        copies, own = exchange[e]
        own.wait()
        for c in copies:
            c.wait_recv()

    ring = {}

    def ring_start(e):
        kind, j, row, rows = MOVES[e]
        arrived(e)
        block = buffers[kind].at[j, y, pl.ds(row, rows)]
        copies = []
        for m, to in enumerate((up, down)):
            copies.append(remote(block, block, y_send.at[e, m], y_recv.at[e, m], to))
            copies[-1].start()
        ring[e] = copies

    def ring_forward(e):
        kind, j, row, rows = MOVES[e]
        copies = ring[e]
        for m, (source, to) in enumerate(((y_down, up), (y_up, down))):
            copies[m].wait_recv()
            block = buffers[kind].at[j, source, pl.ds(row + m * (rows // 2), rows // 2)]
            copies[m] = remote(block, block, y_send.at[e, 2 + m], y_recv.at[e, 2 + m], to)
            copies[m].start()

    def ring_finish(e):
        for c in ring[e]:
            c.wait_recv()

    queries = {}

    def query_start(j):
        arrived(8 + j)
        a = remote(q_buf.at[j, mine], q_buf.at[j, mine], q_send.at[j, 1], q_recv.at[j, 1], partner)
        b = remote(q_buf.at[j, mine], q_buf.at[j, mine], q_send.at[j, 0], q_recv.at[j, 0], sibling)
        a.start()
        b.start()
        queries[j] = [a, b]

    def query_forward(j):
        a, b = queries[j]
        a.wait_recv()
        there = q_buf.at[j, partner_slot]
        c = remote(there, there, q_send.at[j, 2], q_recv.at[j, 2], sibling)
        c.start()
        queries[j] = [b, c]

    def query_finish(j):
        for c in queries[j]:
            c.wait_recv()

    def score(j):
        def one(g, carry):
            for u in range(8):
                hh = g * 8 + u
                lanes = pl.ds(pl.multiple_of(hh * HD, HD), HD)
                q = q_buf[j, :, :, lanes].reshape(TILE, HD)
                k = k_buf[j, :, :, lanes].reshape(TILE, HD)
                scores[(hh // 2) * PARTS + 2 * j + hh % 2] = lax.dot_general(
                    q, k, (((1,), (1,)), ((), ())), preferred_element_type=F32
                )
            return carry

        lax.fori_loop(0, HEADS // 16, one, 0)

    lane = lax.broadcasted_iota(jnp.int32, (MIX, 128), 1)
    minor = lax.broadcasted_iota(jnp.int32, (SLAB, 1), 0)
    per_slot = GROUP_ROWS // SLAB

    logits_of = (logits_even, logits_odd)

    def slab_rows(step, u):
        group, slot = divmod(step, 4)
        first = slot * ROWS + group * GROUP_ROWS + u * SLAB
        return slice(first, first + SLAB)

    def premix(step):
        x = jnp.concatenate(
            [scores[:, slab_rows(step, u), :].reshape(MIX, TILE) for u in range(per_slot)], axis=1
        )
        high, low = split(x)
        logits_of[step % 2][...] = dot(pre_high[...], high) + dot(pre_low[...], high) + dot(pre_high[...], low)

    def softmax_step(step):
        group, slot = divmod(step, 4)
        stats = stat[group]
        for u in range(per_slot):
            i = slot * per_slot + u
            inside = group * GROUP_ROWS + u * SLAB
            span = ((slot // 2) * 8 + y * 2 + slot % 2) * 2 + inside // SPAN
            seen = key_pos[...] <= span_place[span] * SPAN + inside % SPAN + minor
            logits = logits_of[step % 2][:, u * TILE:(u + 1) * TILE].reshape(HEADS, SLAB, TILE)
            masked = jnp.where(seen[None], logits, FLOOR).reshape(MIX, TILE)
            top = jnp.max(masked, axis=1, keepdims=True)
            e = jnp.exp(masked - top)
            total = jnp.sum(e, axis=1, keepdims=True)
            scores[:, slab_rows(step, u), :] = e.reshape(HEADS, SLAB, TILE)
            stats = jnp.where(lane == i, top, jnp.where(lane == i + GROUP_SLABS, total, stats))
        stat[group] = stats

    def softmax(first, last):
        if first == 0:
            premix(0)
        for step in range(first, last):
            if step + 1 < 4 * GROUPS:
                premix(step + 1)
            softmax_step(step)

    stat_copies = {}

    def stat_start(group):
        packed = stat[group, 0:64, :]
        for q in range(1, 4):
            packed += pltpu.roll(stat[group, q * 64:(q + 1) * 64, :], q * 32, 1)
        stat_out[group] = packed
        copies = []
        for n, to in enumerate((sibling, partner, diagonal)):
            copies.append(
                remote(
                    stat_out.at[group], stat_in.at[group, n],
                    stat_send.at[group, n], stat_recv.at[group, n], to,
                )
            )
            copies[-1].start()
        stat_copies[group] = copies

    def stat_finish(group):
        for c in stat_copies[group]:
            c.wait_recv()
        own = stat_out[group]
        others = [stat_in[group, n] for n in range(3)]
        top = functools.reduce(jnp.maximum, others, own)
        total = sum(jnp.exp(s - top) * pltpu.roll(s, 128 - GROUP_SLABS, 1) for s in [own] + others)
        weights = jnp.exp(own - top) / total
        stat[group, 0:64, :] = weights
        for q in range(1, 4):
            stat[group, q * 64:(q + 1) * 64, :] = pltpu.roll(weights, 128 - q * 32, 1)

    far, near = 1 - xh, xh

    def post(group, pair):
        slabs = [pair * 2 * per_slot + u for u in range(2 * per_slot)]
        rows = [
            pl.ds(
                pl.multiple_of(
                    (pair * 2 + u // per_slot) * ROWS + group * GROUP_ROWS + (u % per_slot) * SLAB, SLAB
                ),
                SLAB,
            )
            for u in range(2 * per_slot)
        ]
        weights = stat[group]
        probs = []
        for i, r in zip(slabs, rows):
            weight = jnp.sum(jnp.where(lane == i, weights, 0.0), axis=1, keepdims=True)
            probs.append((scores[:, r, :].reshape(MIX, TILE) * weight).astype(BF16))
        probs = jnp.concatenate(probs, axis=1)
        mixed = dot(post_high[...], probs) + dot(post_low[...], probs)
        for u, r in enumerate(rows):
            scores[:, r, :] = mixed[:, u * TILE:(u + 1) * TILE].reshape(HEADS, SLAB, TILE)

    def attend(j, pair):
        rows = pl.ds(pl.multiple_of(pair * 2 * ROWS, 2 * ROWS), 2 * ROWS)

        def one(g, carry):
            for u in range(8):
                t = g * 8 + u
                lanes = slice(t * HD, (t + 1) * HD)
                v = v_buf[j, :, :, lanes].reshape(TILE, HD)
                m = scores[t * PARTS + j, rows, :].astype(BF16)
                part[j, pl.ds(pair * 2, 2), :, lanes] = dot(m, v).reshape(2, ROWS, HD).astype(BF16)
            return carry

        one(0, 0)

    partial = {}

    def partial_start(j, n):
        slot = (diagonal_slot, sibling_slot)[n]
        partial[j, n] = remote(part.at[j, slot], part_in.at[j, n], p_send.at[j, n], p_recv.at[j, n], sibling)
        partial[j, n].start()

    def attend_far(j):
        attend(j, far)
        partial_start(j, 0)

    def attend_near(j):
        attend(j, near)
        partial_start(j, 1)

    def partial_cross(j):
        partial[j, 0].wait_recv()
        both = part.at[j, partner_slot]
        both[...] = (both[...].astype(F32) + part_in[j, 0].astype(F32)).astype(BF16)
        partial[j, 2] = remote(both, part_in.at[j, 2], p_send.at[j, 2], p_recv.at[j, 2], partner)
        partial[j, 2].start()

    def partial_finish(j):
        partial[j, 1].wait_recv()
        partial[j, 2].wait_recv()
        done = (
            part[j, mine].astype(F32) + part_in[j, 1].astype(F32) + part_in[j, 2].astype(F32)
        ).astype(BF16)
        for t in range(SEQS):
            head = t * PARTS + j
            out[:, head * HD:(head + 1) * HD] = done[:, t * HD:(t + 1) * HD]

    project(0)
    project(1)
    ring_start(0)
    scatter(8)
    project(2)
    scatter(3)
    ring_start(1)
    ring_start(2)
    project(3)
    scatter(9)
    ring_forward(0)
    ring_forward(1)
    project(4)
    ring_start(3)
    ring_forward(2)
    scatter(4)
    scatter(5)
    project(5)
    scatter(6)
    scatter(7)
    query_start(0)
    query_start(1)
    ring_forward(3)
    ring_start(4)
    query_forward(0)
    ring_start(5)
    ring_finish(0)
    ring_finish(1)
    ring_finish(2)
    query_finish(0)
    score(0)
    query_forward(1)
    ring_finish(3)
    query_finish(1)
    score(1)
    softmax(0, 2)
    ring_start(6)
    ring_start(7)
    softmax(2, 4)
    stat_start(0)
    ring_forward(4)
    softmax(4, 8)
    stat_start(1)
    ring_forward(5)
    softmax(8, 12)
    stat_start(2)
    stat_finish(0)
    post(0, far)
    stat_finish(1)
    post(1, far)
    ring_forward(6)
    stat_finish(2)
    post(2, far)
    ring_finish(4)
    attend_far(0)
    ring_finish(5)
    attend_far(1)
    partial_cross(0)
    ring_forward(7)
    post(0, near)
    partial_cross(1)
    ring_finish(6)
    attend_far(2)
    post(1, near)
    partial_cross(2)
    post(2, near)
    attend_near(0)
    attend_near(1)
    ring_finish(7)
    attend_far(3)
    attend_near(2)
    partial_cross(3)
    attend_near(3)
    partial_finish(0)
    partial_finish(1)
    partial_finish(2)
    partial_finish(3)
    for c in sends:
        c.wait_send()


def local(activations, w_query, w_key, w_value, pre_mix, post_mix, span_place):
    any_spec = pl.BlockSpec(memory_space=pl.ANY)
    vmem = pl.BlockSpec(memory_space=pltpu.VMEM)
    dma = pltpu.SemaphoreType.DMA
    out = pl.pallas_call(
        kernel,
        name="heads",
        out_shape=jax.ShapeDtypeStruct((ROWS, MODEL), BF16),
        in_specs=[any_spec] * 4 + [vmem] * 2 + [pl.BlockSpec(memory_space=pltpu.SMEM)],
        out_specs=vmem,
        scratch_shapes=[
            pltpu.VMEM((ROWS, SEQS, MODEL), BF16),
            pltpu.VMEM((3, MODEL, WIDE), BF16),
            pltpu.VMEM((2, 256, HD), F32),
            pltpu.VMEM((2, 2, SEQS, ROWS, WIDE), BF16),
            pltpu.VMEM((PARTS, SEQS, ROWS, HD), BF16),
            pltpu.VMEM((2, 4, ROWS, 2 * PART), BF16),
            pltpu.VMEM((2, 4, ROWS, 2 * PART), BF16),
            pltpu.VMEM((PARTS, 4, ROWS, PART), BF16),
            pltpu.VMEM((HEADS, TILE, TILE), F32),
            pltpu.VMEM((GROUPS, MIX, 128), F32),
            pltpu.VMEM((GROUPS, MIX // 4, 128), F32),
            pltpu.VMEM((GROUPS, 3, MIX // 4, 128), F32),
            pltpu.VMEM((SLAB, TILE), jnp.int32),
            pltpu.VMEM((MIX, GROUP_SLABS // 4 * TILE), F32),
            pltpu.VMEM((MIX, GROUP_SLABS // 4 * TILE), F32),
            pltpu.VMEM((PARTS, 4, ROWS, PART), BF16),
            pltpu.VMEM((PARTS, 3, ROWS, PART), BF16),
            pltpu.VMEM((MIX, MIX), BF16),
            pltpu.VMEM((MIX, MIX), BF16),
            pltpu.VMEM((MIX, MIX), BF16),
            pltpu.VMEM((MIX, MIX), BF16),
            dma((3,)), dma((len(CHUNKS),)), dma((len(MOVES),)),
            dma((len(MOVES), SEQS - 1)), dma((len(MOVES), SEQS - 1)),
            dma((len(MOVES) - 2, 4)), dma((len(MOVES) - 2, 4)),
            dma((2, 3)), dma((2, 3)),
            dma((GROUPS, 3)), dma((GROUPS, 3)),
            dma((PARTS, 3)), dma((PARTS, 3)),
        ],
        compiler_params=pltpu.CompilerParams(
            collective_id=0, has_side_effects=True, vmem_limit_bytes=60 * 2**20
        ),
        cost_estimate=pl.CostEstimate(flops=30 * 10**9, bytes_accessed=30 * 10**6, transcendentals=5 * 10**6),
    )(activations, w_query, w_key, w_value, pre_mix, post_mix, span_place)
    return out.reshape(ROWS, 1, MODEL)


def solution(mesh):
    placed = (P("ctx", None, None), P(None, "tp"), P(None, "tp"), P(None, "tp"), P(), P(), P())
    return jax.shard_map(
        local, mesh=mesh, in_specs=placed, out_specs=P("ctx", "tp", None), check_vma=False
    )
```
